32 devices in a mesh: dp: 8 (over z, x), tensor: 4 (over y, core).
Axes of the slice: x: 2, y: 2, z: 4, core: 2. Of those that a mesh axis runs over, the one named last changes fastest.
Arguments:
- inputs: bfloat16 [4, 512, 4096], P(None, ('dp', 'tensor')), may hold values from -6 to 6
- membrane: float32 [4, 512, 14336], P(None, 'dp', 'tensor'), may hold values from -6 to 6
- spike_grad: bfloat16 [4, 512, 14336], P(None, 'dp', 'tensor'), may hold values from -6 to 6
- decay: float32 [14336], P('tensor'), may hold values from 0.2 to 0.9
- gate_weight: bfloat16 [4096, 14336], P('dp', 'tensor'), may hold values from -0.09375 to 0.09375
Outputs:
- input_grad: bfloat16 [4, 512, 4096], P(None, ('dp', 'tensor'))
- weight_grad: bfloat16 [4096, 14336], P('dp', 'tensor')
The draws below stay inside these ranges and needn't reach their ends.
All inputs are finite; a program needn't handle non-finite values.
Results may differ from the reference program's by a relative error of at most 0.022.
Values may be sent and summed in bfloat16 or wider, within the bound.
A program may use at most 192 MiB of HBM per device.

```python
import math
import jax
import jax.numpy as jnp
from jax import lax

D = 4096
FF = 14336
S = 4
TOK_DEV = 64
TOKENS = 512
N_DP = 8
N_TENSOR = 4


def strengthened(drawn, key, source, target, blocks, factor):
    owner, partner = [(jnp.arange(drawn.shape[axis_at]) // (drawn.shape[axis_at] // blocks)).reshape([-1 if axis == axis_at else 1 for axis in range(drawn.ndim)]) for axis_at in (source, target)]
    chosen = jax.random.permutation(key, blocks)[partner]
    strong = (owner == chosen) | (owner == (partner + blocks // 2) % blocks)
    return jnp.where(strong, factor * drawn, drawn)


def shard_levels(stream_key, dims, shards, smallest, high):
    gain, own = 1.0, jax.random.fold_in(stream_key, 6)
    for dim, shards_of in shards:
        heights = jnp.exp(jax.random.uniform(jax.random.fold_in(own, dim), (shards_of,), jnp.float32, smallest / len(shards), high / len(shards)))
        gain = gain * jnp.repeat(heights, dims[dim] // shards_of).reshape([-1 if axis == dim else 1 for axis in range(len(dims))])
    return gain


def normal_values(key, shape, width, most, shards=(), kind=jnp.bfloat16):
    values = jax.random.normal(key, shape, jnp.float32) * width
    if len(shards) > 0:
        values = shard_levels(key, shape, shards, -0.22, 0.18) * values
    return jnp.clip(values, min=-most, max=most).astype(kind)


def noise_with(key, dims, width, limit, pieces, heavy, held_as=jnp.bfloat16):
    entries = width * jax.random.normal(key, dims, jnp.float32)
    if pieces:
        entries = entries * shard_levels(key, dims, pieces, -0.22, 0.18)
    return jnp.clip(strengthened(entries, jax.random.fold_in(key, 3), *heavy), -limit, limit).astype(held_as)


def setup_inputs(seed: int = 0) -> dict:
    splits = jax.random.split(jax.random.key(seed), 6)
    inputs = noise_with(splits[0], (S, TOKENS, D), 1.0, 6.0, ((1, 32),), (1, 2, 32, 2.75))
    membrane = normal_values(splits[1], (S, TOKENS, FF), 1.0, 6.0, ((1, 8), (2, 4)), jnp.float32)
    spike_grad = noise_with(splits[2], (S, TOKENS, FF), 1.0, 6.0, ((1, 8), (2, 4)), (2, 1, 8, 2.0))
    decay = jnp.clip(jnp.exp(math.log(0.9) - 1.50407736 * jax.random.uniform(splits[3], (FF,), jnp.float32) ** shard_levels(splits[3], (FF,), ((0, 4),), -0.2, 0.2)), 0.2, 0.9)
    gate_weight = normal_values(splits[4], (D, FF), D ** -0.5, 0.09375, ((0, 8), (1, 4)))
    return {"inputs": inputs, "membrane": membrane, "spike_grad": spike_grad, "decay": decay, "gate_weight": gate_weight}


surrogate_slope = 2.0
fire_level = 0.5


def unit_gradients(membrane, spike_grad, decay):
    scaled = surrogate_slope * (membrane - fire_level)
    logistic = jax.nn.sigmoid(scaled)
    surrogate = surrogate_slope * logistic * (1.0 - logistic)
    local_terms = spike_grad.astype(jnp.float32) * surrogate
    carried = jnp.zeros_like(local_terms[0])
    results = []
    for step in reversed(range(local_terms.shape[0])):
        carried = local_terms[step] + decay * carried
        results.append(carried)
    return jnp.stack(results[::-1]).astype(jnp.bfloat16)


def reference(inputs, membrane, spike_grad, decay, gate_weight):
    unit_grad = unit_gradients(membrane, spike_grad, decay)
    grads_wide = unit_grad.astype(jnp.float32)
    inputs_wide = inputs.astype(jnp.float32)
    weight_wide = gate_weight.astype(jnp.float32)
    block_width = FF // N_TENSOR

    def hidden_block(total, index):
        grads_part = lax.dynamic_slice_in_dim(grads_wide, index * block_width, block_width, 2)
        weight_part = lax.dynamic_slice_in_dim(weight_wide, index * block_width, block_width, 1)
        partial_sum = jnp.einsum("stf,df->std", grads_part, weight_part)
        rounded = lax.optimization_barrier(partial_sum.astype(jnp.bfloat16))
        return total + rounded.astype(jnp.float32), None

    input_total, _ = lax.scan(hidden_block, jnp.zeros((S, TOKENS, D), jnp.float32),
                              jnp.arange(N_TENSOR, dtype=jnp.int32))

    def token_block(total, index):
        inputs_part = lax.dynamic_slice_in_dim(inputs_wide, index * TOK_DEV, TOK_DEV, 1)
        grads_part = lax.dynamic_slice_in_dim(grads_wide, index * TOK_DEV, TOK_DEV, 1)
        partial_sum = jnp.einsum("std,stf->df", inputs_part, grads_part)
        rounded = lax.optimization_barrier(partial_sum.astype(jnp.bfloat16))
        return total + rounded.astype(jnp.float32), None

    weight_total, _ = lax.scan(token_block, jnp.zeros((D, FF), jnp.float32),
                               jnp.arange(N_DP, dtype=jnp.int32))
    input_grad = input_total.astype(jnp.bfloat16)
    weight_grad = (weight_total / N_DP).astype(jnp.bfloat16)
    return input_grad, weight_grad
```

```python
import jax
import jax.numpy as jnp
from jax import lax
from jax.sharding import PartitionSpec as P

surrogate_slope = 2.0
fire_level = 0.5


def unit_gradients(membrane, spike_grad, decay):
    scaled = surrogate_slope * (membrane - fire_level)
    logistic = jax.nn.sigmoid(scaled)
    surrogate = surrogate_slope * logistic * (1.0 - logistic)
    local_terms = spike_grad.astype(jnp.float32) * surrogate
    carried = jnp.zeros_like(local_terms[0])
    results = []
    for step in reversed(range(local_terms.shape[0])):
        carried = local_terms[step] + decay * carried
        results.append(carried)
    return jnp.stack(results[::-1]).astype(jnp.bfloat16)


def body(inputs, membrane, spike_grad, decay, gate_weight):
    dp_count = lax.axis_size("dp")
    tensor_count = lax.axis_size("tensor")
    steps, own, features = inputs.shape
    rows = features // dp_count
    unit_grad = unit_gradients(membrane, spike_grad, decay)
    tokens, hidden = unit_grad.shape[1:]
    units = lax.all_gather(
        unit_grad.reshape(steps * tokens, hidden), "dp", axis=0, tiled=True
    )
    columns = inputs.reshape(steps * own, dp_count, rows).transpose(1, 0, 2)
    columns = lax.all_to_all(columns, "dp", split_axis=0, concat_axis=0, tiled=True)
    columns = columns.reshape(dp_count * steps, own, rows)
    columns = lax.all_gather(columns, "tensor", axis=1, tiled=True)
    columns = columns.reshape(dp_count * steps * tokens, rows)
    partial = lax.dot_general(
        units, gate_weight, (((1,), (1,)), ((), ())), preferred_element_type=jnp.float32
    ).astype(jnp.bfloat16)
    partial = partial.reshape(dp_count * steps, tokens, rows)
    partial = lax.psum_scatter(partial, "tensor", scatter_dimension=1, tiled=True)
    partial = partial.reshape(dp_count, steps * own, rows)
    arrived = lax.all_to_all(partial, "dp", split_axis=0, concat_axis=0, tiled=True)
    input_grad = arrived.transpose(1, 0, 2).reshape(steps, own, features)
    weight_grad = lax.dot_general(
        columns, units, (((0,), (0,)), ((), ())), preferred_element_type=jnp.float32
    )
    weight_grad = (weight_grad / dp_count).astype(jnp.bfloat16)
    return (input_grad, weight_grad)


def solution(mesh):
    return jax.shard_map(
        body,
        mesh=mesh,
        in_specs=(
            P(None, ("dp", "tensor"), None),
            P(None, "dp", "tensor"),
            P(None, "dp", "tensor"),
            P("tensor"),
            P("dp", "tensor"),
        ),
        out_specs=(P(None, ("dp", "tensor"), None), P("dp", "tensor")),
        check_vma=False,
    )
```

```python
import functools

import jax
import jax.numpy as jnp
from jax import lax
from jax.experimental import pallas as pl
from jax.experimental.pallas import tpu as pltpu
from jax.sharding import PartitionSpec as P

surrogate_slope = 2.0
fire_level = 0.5
MESH = pl.DeviceIdType.MESH
X = 2
TILES = 7


def unit_gradients(membrane, spike_grad, decay):
    scaled = surrogate_slope * (membrane - fire_level)
    logistic = jax.nn.sigmoid(scaled)
    surrogate = surrogate_slope * logistic * (1.0 - logistic)
    local_terms = spike_grad.astype(jnp.float32) * surrogate
    carried = jnp.zeros_like(local_terms[0])
    results = []
    for step in reversed(range(local_terms.shape[0])):
        carried = local_terms[step] + decay * carried
        results.append(carried)
    return jnp.stack(results[::-1]).astype(jnp.bfloat16)


def kernel(
    DP, T,
    inp, unit, gate, ig_out, wg_out,
    units, cols, weight, total, acc, part, arrived, reduced, grads, wide,
    loc, in1_s, in1_r, in2_s, in2_r, u_r, z_s, d_s, x_s, p_s, p_r, g_s, g_r,
):
    dp, t = lax.axis_index("dp"), lax.axis_index("tensor")
    Z = DP // X
    z, x = dp // X, dp % X
    R = gate.shape[0]
    F = gate.shape[1]
    W = F // TILES

    def remote(src, dst, ss, rs, d, tt):
        return pltpu.make_async_remote_copy(
            src_ref=src, dst_ref=dst, send_sem=ss, recv_sem=rs,
            device_id=(d, tt), device_id_type=MESH,
        )

    def wait(ref, sem):
        pltpu.make_async_copy(ref, ref, sem).wait()

    def columns(ref, d):
        return ref.at[:, pl.ds(pl.multiple_of(d * R, R), R)]

    own_w = pltpu.make_async_copy(gate, weight, loc.at[0])
    own_u = pltpu.make_async_copy(unit, units.at[dp], loc.at[1])
    own_c = pltpu.make_async_copy(columns(inp, dp), cols.at[dp, t], loc.at[2])
    own_w.start()
    own_u.start()
    own_c.start()

    barrier = pltpu.get_barrier_semaphore()

    @pl.loop(1, DP)
    def _(i):
        pl.semaphore_signal(barrier, inc=1, device_id=((dp + i) % DP, t), device_id_type=MESH)

    @pl.loop(1, T)
    def _(i):
        pl.semaphore_signal(barrier, inc=1, device_id=(dp, (t + i) % T), device_id_type=MESH)

    pl.semaphore_wait(barrier, DP + T - 2)

    def in1(d, source):
        return remote(columns(inp, d), cols.at[source, t], in1_s.at[d], in1_r.at[source], d, t)

    @pl.loop(1, DP)
    def _(i):
        in1((dp + i) % DP, dp).start()

    def up(b):
        return remote(units.at[b], units.at[b], z_s.at[b], u_r.at[b], dp + X, t)

    def down(b):
        return remote(units.at[b], units.at[b], d_s.at[b], u_r.at[b], dp - X, t)

    def cross(b):
        return remote(units.at[b], units.at[b], x_s.at[b], u_r.at[b], z * X + (1 - x), t)

    own_u.wait()

    @pl.when(z < Z - 1)
    def _():
        up(dp).start()

    @pl.when(z > 0)
    def _():
        down(dp).start()

    cross(dp).start()

    total[...] = jnp.zeros_like(total)
    own_w.wait()
    own_c.wait()

    @pl.loop(1, DP)
    def _(i):
        b = (dp + i) % DP
        wait(cols.at[b, t], in1_r.at[b])

    def in2(peer, source):
        return remote(cols.at[:, t], cols.at[:, t], in2_s.at[peer], in2_r.at[t], dp, peer)

    @pl.loop(1, T)
    def _(i):
        in2((t + i) % T, t).start()

    @pl.loop(1, T)
    def _(i):
        s = (t + i) % T
        wait(cols.at[:, s], in2_r.at[s])

    rows = unit.shape[0]
    own = rows // T

    def compute(b):
        acc[...] = jnp.zeros_like(acc)
        a = cols[b].reshape(rows, R)

        @pl.loop(0, TILES)
        def _(j):
            tile = pl.ds(pl.multiple_of(j * W, W), W)
            u = units[b, :, tile]
            acc[...] += lax.dot_general(
                u, weight[:, tile], (((1,), (1,)), ((), ())), preferred_element_type=jnp.float32
            )
            total[:, tile] += lax.dot_general(
                a, u, (((0,), (0,)), ((), ())), preferred_element_type=jnp.float32
            )

        part[b] = acc[...].astype(jnp.bfloat16).reshape(T, own, R)

        @pl.loop(1, T)
        def _(i):
            peer = (t + i) % T
            remote(part.at[b, peer], arrived.at[b, i - 1], p_s.at[b], p_r.at[b], dp, peer).start()

    def reduce(b):
        wait(arrived.at[b], p_r.at[b])
        value = part[b, t].astype(jnp.float32)
        for i in range(T - 1):
            value += arrived[b, i].astype(jnp.float32)
        reduced[b] = value.astype(jnp.bfloat16)

        @pl.when(b != dp)
        def _():
            remote(reduced.at[b], columns(grads, dp), g_s.at[b], g_r.at[dp], b, t).start()

        @pl.when(b == dp)
        def _():
            pltpu.make_async_copy(reduced.at[b], columns(grads, dp), g_s.at[b]).start()

    def sides(k, do, column):
        @pl.when((k >= 0) & (k < Z) & (z - k >= 0))
        def _():
            do((z - k) * X + column)

        @pl.when((k > 0) & (z + k < Z))
        def _():
            do((z + k) * X + column)

    def take(b):
        @pl.when(b != dp)
        def _():
            wait(units.at[b], u_r.at[b])

            @pl.when((b < dp) & (z < Z - 1))
            def _():
                up(b).start()

            @pl.when((b > dp) & (z > 0))
            def _():
                down(b).start()

            cross(b).start()

    def take_across(b):
        wait(units.at[b], u_r.at[b])
        compute(b)

    @pl.loop(0, Z + 2)
    def _(k):
        sides(k, take, x)
        sides(k, compute, x)
        sides(k - 1, take_across, 1 - x)
        sides(k - 1, reduce, x)
        sides(k - 2, reduce, 1 - x)

    out_tiles = TILES

    @pl.loop(0, out_tiles)
    def _(j):
        tile = pl.ds(pl.multiple_of(j * W, W), W)
        wide[:, tile] = (total[:, tile] / DP).astype(jnp.bfloat16)

    out_w = pltpu.make_async_copy(wide, wg_out, loc.at[0])
    out_w.start()

    @pl.loop(0, DP)
    def _(b):
        @pl.when(b != dp)
        def _():
            wait(columns(grads, b), g_r.at[b])

        wait(reduced.at[b], g_s.at[b])
        wait(arrived.at[b], p_s.at[b])

    out_i = pltpu.make_async_copy(grads, ig_out, loc.at[1])
    out_i.start()

    @pl.loop(1, DP)
    def _(i):
        wait(cols.at[0, 0], in1_s.at[(dp + i) % DP])

    @pl.loop(1, T)
    def _(i):
        wait(cols.at[:, 0], in2_s.at[(t + i) % T])

    @pl.loop(0, Z)
    def _(c):
        b = c * X + x
        wait(units.at[b], x_s.at[b])

        @pl.when((c <= z) & (z < Z - 1))
        def _():
            wait(units.at[b], z_s.at[b])

        @pl.when((c >= z) & (z > 0))
        def _():
            wait(units.at[b], d_s.at[b])

    out_w.wait()
    out_i.wait()


def body(inputs, membrane, spike_grad, decay, gate_weight):
    DP, T = lax.axis_size("dp"), lax.axis_size("tensor")
    steps, own, features = inputs.shape
    R, F = gate_weight.shape
    unit_grad = unit_gradients(membrane, spike_grad, decay)
    rows = steps * own * T
    unit = unit_grad.reshape(steps, T, own, F).transpose(1, 0, 2, 3).reshape(rows, F)
    inp = inputs.reshape(steps * own, features)
    bf, f32 = jnp.bfloat16, jnp.float32
    dma = pltpu.SemaphoreType.DMA
    ig, wg = pl.pallas_call(
        functools.partial(kernel, DP, T),
        out_shape=(
            jax.ShapeDtypeStruct((steps * own, features), bf),
            jax.ShapeDtypeStruct((R, F), bf),
        ),
        in_specs=[pl.BlockSpec(memory_space=pl.ANY)] * 3,
        out_specs=(pl.BlockSpec(memory_space=pl.ANY),) * 2,
        scratch_shapes=[
            pltpu.VMEM((DP, rows, F), bf),
            pltpu.VMEM((DP, T, rows // T, R), bf),
            pltpu.VMEM((R, F), bf),
            pltpu.VMEM((R, F), f32),
            pltpu.VMEM((rows, R), f32),
            pltpu.VMEM((DP, T, rows // T, R), bf),
            pltpu.VMEM((DP, T - 1, rows // T, R), bf),
            pltpu.VMEM((DP, rows // T, R), bf),
            pltpu.VMEM((steps * own, features), bf),
            pltpu.VMEM((R, F), bf),
            dma((3,)), dma((DP,)), dma((DP,)), dma((T,)), dma((T,)),
            dma((DP,)), dma((DP,)), dma((DP,)), dma((DP,)),
            dma((DP,)), dma((DP,)), dma((DP,)), dma((DP,)),
        ],
        compiler_params=pltpu.CompilerParams(
            collective_id=0, has_side_effects=True, vmem_limit_bytes=56 * 1024 * 1024
        ),
        cost_estimate=pl.CostEstimate(
            flops=4 * DP * rows * R * F, bytes_accessed=4 * R * F + 2 * rows * F, transcendentals=0
        ),
    )(inp, unit, gate_weight)
    return (ig.reshape(steps, own, features), wg)


def solution(mesh):
    return jax.shard_map(
        body,
        mesh=mesh,
        in_specs=(
            P(None, ("dp", "tensor"), None),
            P(None, "dp", "tensor"),
            P(None, "dp", "tensor"),
            P("tensor"),
            P("dp", "tensor"),
        ),
        out_specs=(P(None, ("dp", "tensor"), None), P("dp", "tensor")),
        check_vma=False,
    )
```

```python
import functools

import jax
import jax.numpy as jnp
from jax import lax
from jax.experimental import pallas as pl
from jax.experimental.pallas import tpu as pltpu
from jax.sharding import PartitionSpec as P

surrogate_slope = 2.0
fire_level = 0.5
MESH = pl.DeviceIdType.MESH
X = 2
TILES = 7


def unit_gradients(membrane, spike_grad, decay):
    scaled = surrogate_slope * (membrane - fire_level)
    logistic = jax.nn.sigmoid(scaled)
    surrogate = surrogate_slope * logistic * (1.0 - logistic)
    local_terms = spike_grad.astype(jnp.float32) * surrogate
    carried = jnp.zeros_like(local_terms[0])
    results = []
    for step in reversed(range(local_terms.shape[0])):
        carried = local_terms[step] + decay * carried
        results.append(carried)
    return jnp.stack(results[::-1]).astype(jnp.bfloat16)


def kernel(
    DP, T,
    inp, unit, gate, ig_out, wg_out,
    units, cols, weight, total, acc, part, arrived, reduced, grads, wide,
    loc, in1_s, in1_r, in2_s, in2_r, u_r, v_r, z_s, d_s, b_s, x_s, p_s, p_r, g_s, g_r,
):
    dp, t = lax.axis_index("dp"), lax.axis_index("tensor")
    Z = DP // X
    z, x = dp // X, dp % X
    R = gate.shape[0]
    F = gate.shape[1]
    W = F // TILES

    def remote(src, dst, ss, rs, d, tt):
        return pltpu.make_async_remote_copy(
            src_ref=src, dst_ref=dst, send_sem=ss, recv_sem=rs,
            device_id=(d, tt), device_id_type=MESH,
        )

    def wait(ref, sem):
        pltpu.make_async_copy(ref, ref, sem).wait()

    def columns(ref, d):
        return ref.at[:, pl.ds(pl.multiple_of(d * R, R), R)]

    own_w = pltpu.make_async_copy(gate, weight, loc.at[0])
    own_u = pltpu.make_async_copy(unit, units.at[dp], loc.at[1])
    own_c = pltpu.make_async_copy(columns(inp, dp), cols.at[dp, t], loc.at[2])
    own_w.start()
    own_u.start()
    own_c.start()

    barrier = pltpu.get_barrier_semaphore()

    @pl.loop(1, DP)
    def _(i):
        pl.semaphore_signal(barrier, inc=1, device_id=((dp + i) % DP, t), device_id_type=MESH)

    @pl.loop(1, T)
    def _(i):
        pl.semaphore_signal(barrier, inc=1, device_id=(dp, (t + i) % T), device_id_type=MESH)

    pl.semaphore_wait(barrier, DP + T - 2)

    def in1(d, source):
        return remote(columns(inp, d), cols.at[source, t], in1_s.at[d], in1_r.at[source], d, t)

    @pl.loop(1, DP)
    def _(i):
        in1((dp + i) % DP, dp).start()

    rows = unit.shape[0]
    own = rows // T
    half = rows // 2

    def whole(b):
        return units.at[b]

    def first(b):
        return units.at[b, pl.ds(0, half)]

    def second(b):
        return units.at[b, pl.ds(half, half)]

    def up(ref, b, ss=z_s, rs=u_r):
        remote(ref, ref, ss.at[b], rs.at[b], dp + X, t).start()

    def down(ref, b, ss=d_s, rs=u_r):
        remote(ref, ref, ss.at[b], rs.at[b], dp - X, t).start()

    def cross(ref, b):
        remote(ref, ref, x_s.at[b], u_r.at[b], z * X + (1 - x), t).start()

    def is_end(b):
        return (b < X) | (b >= DP - X)

    own_u.wait()

    @pl.when(z == 0)
    def _():
        up(first(dp), dp)
        cross(whole(dp), dp)
        up(second(dp), dp, b_s, v_r)

    @pl.when(z == Z - 1)
    def _():
        down(first(dp), dp)
        cross(whole(dp), dp)
        down(second(dp), dp, b_s, v_r)

    @pl.when((z > 0) & (z < Z - 1))
    def _():
        up(whole(dp), dp)
        down(whole(dp), dp)
        cross(whole(dp), dp)

    total[...] = jnp.zeros_like(total)
    own_w.wait()
    own_c.wait()

    @pl.loop(1, DP)
    def _(i):
        b = (dp + i) % DP
        wait(cols.at[b, t], in1_r.at[b])

    def in2(peer, source):
        return remote(cols.at[:, t], cols.at[:, t], in2_s.at[peer], in2_r.at[t], dp, peer)

    @pl.loop(1, T)
    def _(i):
        in2((t + i) % T, t).start()

    @pl.loop(1, T)
    def _(i):
        s = (t + i) % T
        wait(cols.at[:, s], in2_r.at[s])

    def compute(b):
        acc[...] = jnp.zeros_like(acc)
        a = cols[b].reshape(rows, R)

        @pl.loop(0, TILES)
        def _(j):
            tile = pl.ds(pl.multiple_of(j * W, W), W)
            u = units[b, :, tile]
            acc[...] += lax.dot_general(
                u, weight[:, tile], (((1,), (1,)), ((), ())), preferred_element_type=jnp.float32
            )
            total[:, tile] += lax.dot_general(
                a, u, (((0,), (0,)), ((), ())), preferred_element_type=jnp.float32
            )

        part[b] = acc[...].astype(jnp.bfloat16).reshape(T, own, R)

        @pl.loop(1, T)
        def _(i):
            peer = (t + i) % T
            remote(part.at[b, peer], arrived.at[b, i - 1], p_s.at[b], p_r.at[b], dp, peer).start()

    def reduce(b):
        wait(arrived.at[b], p_r.at[b])
        value = part[b, t].astype(jnp.float32)
        for i in range(T - 1):
            value += arrived[b, i].astype(jnp.float32)
        reduced[b] = value.astype(jnp.bfloat16)

        @pl.when(b != dp)
        def _():
            remote(reduced.at[b], columns(grads, dp), g_s.at[b], g_r.at[dp], b, t).start()

        @pl.when(b == dp)
        def _():
            pltpu.make_async_copy(reduced.at[b], columns(grads, dp), g_s.at[b]).start()

    def sides(k, do, column):
        @pl.when((k >= 0) & (k < Z) & (z - k >= 0))
        def _():
            do((z - k) * X + column)

        @pl.when((k > 0) & (z + k < Z))
        def _():
            do((z + k) * X + column)

    def forward(ref, b, up_s=z_s, down_s=d_s, rs=u_r):
        @pl.when((b < z * X) & (z < Z - 1))
        def _():
            up(ref, b, up_s, rs)

        @pl.when((b >= (z + 1) * X) & (z > 0))
        def _():
            down(ref, b, down_s, rs)

    def take(b):
        @pl.when((b != dp) & is_end(b))
        def _():
            wait(first(b), u_r.at[b])
            forward(first(b), b)
            cross(first(b), b)

        @pl.when((b != dp) & jnp.logical_not(is_end(b)))
        def _():
            wait(whole(b), u_r.at[b])
            forward(whole(b), b)
            cross(whole(b), b)

    def is_split(b):
        return is_end(b) & (b // X != z)

    def compute_whole(b):
        @pl.when(jnp.logical_not(is_split(b)))
        def _():
            compute(b)

    def across_whole(b):
        @pl.when(jnp.logical_not(is_split(b)))
        def _():
            wait(whole(b), u_r.at[b])

            @pl.when(z == 0)
            def _():
                @pl.when(b < X)
                def _():
                    up(second(b), b, b_s, v_r)

            @pl.when(z == Z - 1)
            def _():
                @pl.when(b >= DP - X)
                def _():
                    down(second(b), b, b_s, v_r)

            compute(b)

    def take_second(b):
        @pl.when(is_split(b))
        def _():
            wait(second(b), v_r.at[b])
            forward(second(b), b, b_s, b_s, v_r)

    def compute_split(b):
        @pl.when(is_split(b))
        def _():
            compute(b)

    def across_split(b):
        @pl.when(is_split(b))
        def _():
            wait(first(b), u_r.at[b])
            compute(b)

    @pl.loop(0, Z + 2)
    def _(k):
        sides(k, take, x)
        sides(k, compute_whole, x)
        sides(k - 1, across_whole, 1 - x)
        sides(k, take_second, x)
        sides(k, take_second, 1 - x)
        sides(k, compute_split, x)
        sides(k - 1, across_split, 1 - x)
        sides(k - 1, reduce, x)
        sides(k - 2, reduce, 1 - x)

    out_tiles = TILES

    @pl.loop(0, out_tiles)
    def _(j):
        tile = pl.ds(pl.multiple_of(j * W, W), W)
        wide[:, tile] = (total[:, tile] / DP).astype(jnp.bfloat16)

    out_w = pltpu.make_async_copy(wide, wg_out, loc.at[0])
    out_w.start()

    @pl.loop(0, DP)
    def _(b):
        @pl.when(b != dp)
        def _():
            wait(columns(grads, b), g_r.at[b])

        wait(reduced.at[b], g_s.at[b])
        wait(arrived.at[b], p_s.at[b])

    out_i = pltpu.make_async_copy(grads, ig_out, loc.at[1])
    out_i.start()

    @pl.loop(1, DP)
    def _(i):
        wait(cols.at[0, 0], in1_s.at[(dp + i) % DP])

    @pl.loop(1, T)
    def _(i):
        wait(cols.at[:, 0], in2_s.at[(t + i) % T])

    def sent(b, cond, sem, split):
        @pl.when(cond & split)
        def _():
            wait(first(b), sem.at[b])

        @pl.when(cond & jnp.logical_not(split))
        def _():
            wait(whole(b), sem.at[b])

    @pl.loop(0, Z)
    def _(c):
        b = c * X + x
        sent(b, c >= 0, x_s, is_split(b))
        sent(b, (c <= z) & (z < Z - 1), z_s, is_end(b))
        sent(b, (c >= z) & (z > 0), d_s, is_end(b))

    @pl.loop(0, X)
    def _(c):
        @pl.when(z < Z - 1)
        def _():
            wait(second(c), b_s.at[c])

        @pl.when(z > 0)
        def _():
            wait(second(DP - X + c), b_s.at[DP - X + c])

    out_w.wait()
    out_i.wait()


def body(inputs, membrane, spike_grad, decay, gate_weight):
    DP, T = lax.axis_size("dp"), lax.axis_size("tensor")
    steps, own, features = inputs.shape
    R, F = gate_weight.shape
    unit_grad = unit_gradients(membrane, spike_grad, decay)
    rows = steps * own * T
    unit = unit_grad.reshape(steps, T, own, F).transpose(1, 0, 2, 3).reshape(rows, F)
    inp = inputs.reshape(steps * own, features)
    bf, f32 = jnp.bfloat16, jnp.float32
    dma = pltpu.SemaphoreType.DMA
    ig, wg = pl.pallas_call(
        functools.partial(kernel, DP, T),
        out_shape=(
            jax.ShapeDtypeStruct((steps * own, features), bf),
            jax.ShapeDtypeStruct((R, F), bf),
        ),
        in_specs=[pl.BlockSpec(memory_space=pl.ANY)] * 3,
        out_specs=(pl.BlockSpec(memory_space=pl.ANY),) * 2,
        scratch_shapes=[
            pltpu.VMEM((DP, rows, F), bf),
            pltpu.VMEM((DP, T, rows // T, R), bf),
            pltpu.VMEM((R, F), bf),
            pltpu.VMEM((R, F), f32),
            pltpu.VMEM((rows, R), f32),
            pltpu.VMEM((DP, T, rows // T, R), bf),
            pltpu.VMEM((DP, T - 1, rows // T, R), bf),
            pltpu.VMEM((DP, rows // T, R), bf),
            pltpu.VMEM((steps * own, features), bf),
            pltpu.VMEM((R, F), bf),
            dma((3,)), dma((DP,)), dma((DP,)), dma((T,)), dma((T,)),
            dma((DP,)), dma((DP,)), dma((DP,)), dma((DP,)), dma((DP,)), dma((DP,)),
            dma((DP,)), dma((DP,)), dma((DP,)), dma((DP,)),
        ],
        compiler_params=pltpu.CompilerParams(
            collective_id=0, has_side_effects=True, vmem_limit_bytes=56 * 1024 * 1024
        ),
        cost_estimate=pl.CostEstimate(
            flops=4 * DP * rows * R * F, bytes_accessed=4 * R * F + 2 * rows * F, transcendentals=0
        ),
    )(inp, unit, gate_weight)
    return (ig.reshape(steps, own, features), wg)


def solution(mesh):
    return jax.shard_map(
        body,
        mesh=mesh,
        in_specs=(
            P(None, ("dp", "tensor"), None),
            P(None, "dp", "tensor"),
            P(None, "dp", "tensor"),
            P("tensor"),
            P("dp", "tensor"),
        ),
        out_specs=(P(None, ("dp", "tensor"), None), P("dp", "tensor")),
        check_vma=False,
    )
```

```python
import functools

import jax
import jax.numpy as jnp
from jax import lax
from jax.experimental import pallas as pl
from jax.experimental.pallas import tpu as pltpu
from jax.sharding import PartitionSpec as P

surrogate_slope = 2.0
fire_level = 0.5
MESH = pl.DeviceIdType.MESH
X = 2
TILES = 7


def unit_gradients(membrane, spike_grad, decay):
    scaled = surrogate_slope * (membrane - fire_level)
    logistic = jax.nn.sigmoid(scaled)
    surrogate = surrogate_slope * logistic * (1.0 - logistic)
    local_terms = spike_grad.astype(jnp.float32) * surrogate
    carried = jnp.zeros_like(local_terms[0])
    results = []
    for step in reversed(range(local_terms.shape[0])):
        carried = local_terms[step] + decay * carried
        results.append(carried)
    return jnp.stack(results[::-1]).astype(jnp.bfloat16)


def kernel(
    DP, T,
    inp, unit, gate, ig_out, wg_out,
    units, cols, weight, total, acc, part, arrived, reduced, grads, wide,
    loc, in1_s, in1_r, in2_s, in2_r, u_r, v_r, z_s, d_s, b_s, x_s, p_s, p_r, g_s, g_r,
):
    dp, t = lax.axis_index("dp"), lax.axis_index("tensor")
    Z = DP // X
    z, x = dp // X, dp % X
    R = gate.shape[0]
    F = gate.shape[1]
    W = F // TILES

    def remote(src, dst, ss, rs, d, tt):
        return pltpu.make_async_remote_copy(
            src_ref=src, dst_ref=dst, send_sem=ss, recv_sem=rs,
            device_id=(d, tt), device_id_type=MESH,
        )

    def wait(ref, sem):
        pltpu.make_async_copy(ref, ref, sem).wait()

    def columns(ref, d):
        return ref.at[:, pl.ds(pl.multiple_of(d * R, R), R)]

    own_w = pltpu.make_async_copy(gate, weight, loc.at[0])
    own_u = pltpu.make_async_copy(unit, units.at[dp], loc.at[1])
    own_c = pltpu.make_async_copy(columns(inp, dp), cols.at[dp, t], loc.at[2])
    own_w.start()
    own_u.start()
    own_c.start()

    barrier = pltpu.get_barrier_semaphore()

    @pl.loop(1, DP)
    def _(i):
        pl.semaphore_signal(barrier, inc=1, device_id=((dp + i) % DP, t), device_id_type=MESH)

    @pl.loop(1, T)
    def _(i):
        pl.semaphore_signal(barrier, inc=1, device_id=(dp, (t + i) % T), device_id_type=MESH)

    pl.semaphore_wait(barrier, DP + T - 2)

    def in1(d, source):
        return remote(columns(inp, d), cols.at[source, t], in1_s.at[d], in1_r.at[source], d, t)

    @pl.loop(1, DP)
    def _(i):
        in1((dp + i) % DP, dp).start()

    rows = unit.shape[0]
    own = rows // T
    half = rows // 2

    def whole(b):
        return units.at[b]

    def first(b):
        return units.at[b, pl.ds(0, half)]

    def second(b):
        return units.at[b, pl.ds(half, half)]

    def up(ref, b, ss=z_s, rs=u_r):
        remote(ref, ref, ss.at[b], rs.at[b], dp + X, t).start()

    def down(ref, b, ss=d_s, rs=u_r):
        remote(ref, ref, ss.at[b], rs.at[b], dp - X, t).start()

    def cross(ref, b):
        remote(ref, ref, x_s.at[b], u_r.at[b], z * X + (1 - x), t).start()

    def is_end(b):
        return (b < X) | (b >= DP - X)

    own_u.wait()

    @pl.when(z == 0)
    def _():
        up(first(dp), dp)
        cross(whole(dp), dp)

    @pl.when(z == Z - 1)
    def _():
        down(first(dp), dp)
        cross(whole(dp), dp)

    @pl.when((z > 0) & (z < Z - 1))
    def _():
        up(whole(dp), dp)
        down(whole(dp), dp)
        cross(whole(dp), dp)

    total[...] = jnp.zeros_like(total)
    own_w.wait()
    own_c.wait()

    @pl.loop(1, DP)
    def _(i):
        b = (dp + i) % DP
        wait(cols.at[b, t], in1_r.at[b])

    def in2(peer, source):
        return remote(cols.at[:, t], cols.at[:, t], in2_s.at[peer], in2_r.at[t], dp, peer)

    @pl.loop(1, T)
    def _(i):
        in2((t + i) % T, t).start()

    @pl.loop(1, T)
    def _(i):
        s = (t + i) % T
        wait(cols.at[:, s], in2_r.at[s])

    def compute(b):
        acc[...] = jnp.zeros_like(acc)
        a = cols[b].reshape(rows, R)

        @pl.loop(0, TILES)
        def _(j):
            tile = pl.ds(pl.multiple_of(j * W, W), W)
            u = units[b, :, tile]
            acc[...] += lax.dot_general(
                u, weight[:, tile], (((1,), (1,)), ((), ())), preferred_element_type=jnp.float32
            )
            total[:, tile] += lax.dot_general(
                a, u, (((0,), (0,)), ((), ())), preferred_element_type=jnp.float32
            )

        part[b] = acc[...].astype(jnp.bfloat16).reshape(T, own, R)

        @pl.loop(1, T)
        def _(i):
            peer = (t + i) % T
            remote(part.at[b, peer], arrived.at[b, i - 1], p_s.at[b], p_r.at[b], dp, peer).start()

    def reduce(b):
        wait(arrived.at[b], p_r.at[b])
        value = part[b, t].astype(jnp.float32)
        for i in range(T - 1):
            value += arrived[b, i].astype(jnp.float32)
        reduced[b] = value.astype(jnp.bfloat16)

        @pl.when(b != dp)
        def _():
            remote(reduced.at[b], columns(grads, dp), g_s.at[b], g_r.at[dp], b, t).start()

        @pl.when(b == dp)
        def _():
            pltpu.make_async_copy(reduced.at[b], columns(grads, dp), g_s.at[b]).start()

    def sides(k, do, column):
        @pl.when((k >= 0) & (k < Z) & (z - k >= 0))
        def _():
            do((z - k) * X + column)

        @pl.when((k > 0) & (z + k < Z))
        def _():
            do((z + k) * X + column)

    def forward(ref, b, up_s=z_s, down_s=d_s, rs=u_r):
        @pl.when((b < z * X) & (z < Z - 1))
        def _():
            up(ref, b, up_s, rs)

        @pl.when((b >= (z + 1) * X) & (z > 0))
        def _():
            down(ref, b, down_s, rs)

    def take(b):
        @pl.when((b != dp) & is_end(b))
        def _():
            wait(first(b), u_r.at[b])
            forward(first(b), b)
            cross(first(b), b)

        @pl.when((b != dp) & jnp.logical_not(is_end(b)))
        def _():
            wait(whole(b), u_r.at[b])
            forward(whole(b), b)
            cross(whole(b), b)

    def is_split(b):
        return is_end(b) & (b // X != z)

    def compute_whole(b):
        @pl.when(jnp.logical_not(is_split(b)))
        def _():
            compute(b)

    def across_first(b):
        wait(whole(b), u_r.at[b])

        @pl.when(z == 0)
        def _():
            up(second(b), b, b_s, v_r)

        @pl.when(z == Z - 1)
        def _():
            down(second(b), b, b_s, v_r)

    def across_whole(b):
        @pl.when(jnp.logical_not(is_split(b)))
        def _():
            @pl.when(b // X != z)
            def _():
                wait(whole(b), u_r.at[b])

            compute(b)

    def at_last(do):
        def run(b):
            @pl.when((z == 0) | (z == Z - 1))
            def _():
                do(b)
        return run

    def before_last(do):
        def run(b):
            @pl.when((z > 0) & (z < Z - 1))
            def _():
                do(b)
        return run

    def take_second(b):
        @pl.when(is_split(b))
        def _():
            wait(second(b), v_r.at[b])
            forward(second(b), b, b_s, b_s, v_r)

    def compute_split(b):
        @pl.when(is_split(b))
        def _():
            compute(b)

    def across_split(b):
        @pl.when(is_split(b))
        def _():
            wait(first(b), u_r.at[b])
            compute(b)

    @pl.loop(0, Z + 2)
    def _(k):
        sides(k, take, x)

        @pl.when(k == 1)
        def _():
            across_first(z * X + (1 - x))

        sides(k, compute_whole, x)

        @pl.when((k == 0) & (z == 0))
        def _():
            wait(first(dp), z_s.at[dp])
            up(second(dp), dp, b_s, v_r)

        @pl.when((k == 0) & (z == Z - 1))
        def _():
            wait(first(dp), d_s.at[dp])
            down(second(dp), dp, b_s, v_r)

        sides(k - 1, across_whole, 1 - x)
        sides(k, take_second, x)
        sides(k, at_last(compute_split), x)
        sides(k, take_second, 1 - x)
        sides(k, before_last(compute_split), x)
        sides(k - 1, across_split, 1 - x)
        sides(k - 1, reduce, x)
        sides(k - 2, reduce, 1 - x)

    out_tiles = TILES

    @pl.loop(0, out_tiles)
    def _(j):
        tile = pl.ds(pl.multiple_of(j * W, W), W)
        wide[:, tile] = (total[:, tile] / DP).astype(jnp.bfloat16)

    out_w = pltpu.make_async_copy(wide, wg_out, loc.at[0])
    out_w.start()

    @pl.loop(0, DP)
    def _(b):
        @pl.when(b != dp)
        def _():
            wait(columns(grads, b), g_r.at[b])

        wait(reduced.at[b], g_s.at[b])
        wait(arrived.at[b], p_s.at[b])

    out_i = pltpu.make_async_copy(grads, ig_out, loc.at[1])
    out_i.start()

    @pl.loop(1, DP)
    def _(i):
        wait(cols.at[0, 0], in1_s.at[(dp + i) % DP])

    @pl.loop(1, T)
    def _(i):
        wait(cols.at[:, 0], in2_s.at[(t + i) % T])

    def sent(b, cond, sem, split):
        @pl.when(cond & split)
        def _():
            wait(first(b), sem.at[b])

        @pl.when(cond & jnp.logical_not(split))
        def _():
            wait(whole(b), sem.at[b])

    @pl.loop(0, Z)
    def _(c):
        b = c * X + x
        sent(b, c >= 0, x_s, is_split(b))
        sent(b, (c <= z) & (z < Z - 1) & (z + c > 0), z_s, is_end(b))
        sent(b, (c >= z) & (z > 0) & (z + c < 2 * Z - 2), d_s, is_end(b))

    @pl.loop(0, X)
    def _(c):
        @pl.when(z < Z - 1)
        def _():
            wait(second(c), b_s.at[c])

        @pl.when(z > 0)
        def _():
            wait(second(DP - X + c), b_s.at[DP - X + c])

    out_w.wait()
    out_i.wait()


def body(inputs, membrane, spike_grad, decay, gate_weight):
    DP, T = lax.axis_size("dp"), lax.axis_size("tensor")
    steps, own, features = inputs.shape
    R, F = gate_weight.shape
    unit_grad = unit_gradients(membrane, spike_grad, decay)
    rows = steps * own * T
    unit = unit_grad.reshape(steps, T, own, F).transpose(1, 0, 2, 3).reshape(rows, F)
    inp = inputs.reshape(steps * own, features)
    bf, f32 = jnp.bfloat16, jnp.float32
    dma = pltpu.SemaphoreType.DMA
    ig, wg = pl.pallas_call(
        functools.partial(kernel, DP, T),
        out_shape=(
            jax.ShapeDtypeStruct((steps * own, features), bf),
            jax.ShapeDtypeStruct((R, F), bf),
        ),
        in_specs=[pl.BlockSpec(memory_space=pl.ANY)] * 3,
        out_specs=(pl.BlockSpec(memory_space=pl.ANY),) * 2,
        scratch_shapes=[
            pltpu.VMEM((DP, rows, F), bf),
            pltpu.VMEM((DP, T, rows // T, R), bf),
            pltpu.VMEM((R, F), bf),
            pltpu.VMEM((R, F), f32),
            pltpu.VMEM((rows, R), f32),
            pltpu.VMEM((DP, T, rows // T, R), bf),
            pltpu.VMEM((DP, T - 1, rows // T, R), bf),
            pltpu.VMEM((DP, rows // T, R), bf),
            pltpu.VMEM((steps * own, features), bf),
            pltpu.VMEM((R, F), bf),
            dma((3,)), dma((DP,)), dma((DP,)), dma((T,)), dma((T,)),
            dma((DP,)), dma((DP,)), dma((DP,)), dma((DP,)), dma((DP,)), dma((DP,)),
            dma((DP,)), dma((DP,)), dma((DP,)), dma((DP,)),
        ],
        compiler_params=pltpu.CompilerParams(
            collective_id=0, has_side_effects=True, vmem_limit_bytes=56 * 1024 * 1024
        ),
        cost_estimate=pl.CostEstimate(
            flops=4 * DP * rows * R * F, bytes_accessed=4 * R * F + 2 * rows * F, transcendentals=0
        ),
    )(inp, unit, gate_weight)
    return (ig.reshape(steps, own, features), wg)


def solution(mesh):
    return jax.shard_map(
        body,
        mesh=mesh,
        in_specs=(
            P(None, ("dp", "tensor"), None),
            P(None, "dp", "tensor"),
            P(None, "dp", "tensor"),
            P("tensor"),
            P("dp", "tensor"),
        ),
        out_specs=(P(None, ("dp", "tensor"), None), P("dp", "tensor")),
        check_vma=False,
    )
```

```python
import functools

import jax
import jax.numpy as jnp
from jax import lax
from jax.experimental import pallas as pl
from jax.experimental.pallas import tpu as pltpu
from jax.sharding import PartitionSpec as P

surrogate_slope = 2.0
fire_level = 0.5
MESH = pl.DeviceIdType.MESH
X = 2
TILES = 7


def unit_gradients(membrane, spike_grad, decay):
    scaled = surrogate_slope * (membrane - fire_level)
    logistic = jax.nn.sigmoid(scaled)
    surrogate = surrogate_slope * logistic * (1.0 - logistic)
    local_terms = spike_grad.astype(jnp.float32) * surrogate
    carried = jnp.zeros_like(local_terms[0])
    results = []
    for step in reversed(range(local_terms.shape[0])):
        carried = local_terms[step] + decay * carried
        results.append(carried)
    return jnp.stack(results[::-1]).astype(jnp.bfloat16)


def kernel(
    DP, T,
    inp, unit, gate, ig_out, wg_out,
    units, cols, weight, total, acc, part, arrived, reduced, grads, wide,
    loc, in1_s, in1_r, in2_s, in2_r, u_r, v_r, z_s, d_s, b_s, x_s, p_s, p_r, g_s, g_r,
):
    dp, t = lax.axis_index("dp"), lax.axis_index("tensor")
    Z = DP // X
    z, x = dp // X, dp % X
    R = gate.shape[0]
    F = gate.shape[1]
    W = F // TILES

    def remote(src, dst, ss, rs, d, tt):
        return pltpu.make_async_remote_copy(
            src_ref=src, dst_ref=dst, send_sem=ss, recv_sem=rs,
            device_id=(d, tt), device_id_type=MESH,
        )

    def wait(ref, sem):
        pltpu.make_async_copy(ref, ref, sem).wait()

    def columns(ref, d):
        return ref.at[:, pl.ds(pl.multiple_of(d * R, R), R)]

    own_w = pltpu.make_async_copy(gate, weight, loc.at[0])
    own_u = pltpu.make_async_copy(unit, units.at[dp], loc.at[1])
    own_c = pltpu.make_async_copy(columns(inp, dp), cols.at[dp, t], loc.at[2])
    own_w.start()
    own_u.start()
    own_c.start()

    barrier = pltpu.get_barrier_semaphore()

    @pl.loop(1, DP)
    def _(i):
        pl.semaphore_signal(barrier, inc=1, device_id=((dp + i) % DP, t), device_id_type=MESH)

    @pl.loop(1, T)
    def _(i):
        pl.semaphore_signal(barrier, inc=1, device_id=(dp, (t + i) % T), device_id_type=MESH)

    pl.semaphore_wait(barrier, DP + T - 2)

    def in1(d, source):
        return remote(columns(inp, d), cols.at[source, t], in1_s.at[d], in1_r.at[source], d, t)

    @pl.loop(1, DP)
    def _(i):
        in1((dp + i) % DP, dp).start()

    rows = unit.shape[0]
    own = rows // T
    half = rows // 2

    def whole(b):
        return units.at[b]

    def first(b):
        return units.at[b, pl.ds(0, half)]

    def second(b):
        return units.at[b, pl.ds(half, half)]

    def up(ref, b, ss=z_s, rs=u_r):
        remote(ref, ref, ss.at[b], rs.at[b], dp + X, t).start()

    def down(ref, b, ss=d_s, rs=u_r):
        remote(ref, ref, ss.at[b], rs.at[b], dp - X, t).start()

    def cross(ref, b):
        remote(ref, ref, x_s.at[b], u_r.at[b], z * X + (1 - x), t).start()

    def is_end(b):
        return (b < X) | (b >= DP - X)

    own_u.wait()

    @pl.when(z == 0)
    def _():
        up(first(dp), dp)
        cross(whole(dp), dp)

    @pl.when(z == Z - 1)
    def _():
        down(first(dp), dp)
        cross(whole(dp), dp)

    @pl.when((z > 0) & (z < Z - 1))
    def _():
        up(whole(dp), dp)
        down(whole(dp), dp)
        cross(whole(dp), dp)

    total[...] = jnp.zeros_like(total)
    own_w.wait()
    own_c.wait()

    @pl.loop(1, DP)
    def _(i):
        b = (dp + i) % DP
        wait(cols.at[b, t], in1_r.at[b])

    def in2(peer, source):
        return remote(cols.at[:, t], cols.at[:, t], in2_s.at[peer], in2_r.at[t], dp, peer)

    @pl.loop(1, T)
    def _(i):
        in2((t + i) % T, t).start()

    @pl.loop(1, T)
    def _(i):
        s = (t + i) % T
        wait(cols.at[:, s], in2_r.at[s])

    def compute(b):
        acc[...] = jnp.zeros_like(acc)
        a = cols[b].reshape(rows, R)

        @pl.loop(0, TILES)
        def _(j):
            tile = pl.ds(pl.multiple_of(j * W, W), W)
            u = units[b, :, tile]
            acc[...] += lax.dot_general(
                u, weight[:, tile], (((1,), (1,)), ((), ())), preferred_element_type=jnp.float32
            )

        part[b] = acc[...].astype(jnp.bfloat16).reshape(T, own, R)

        @pl.loop(1, T)
        def _(i):
            peer = (t + i) % T
            remote(part.at[b, peer], arrived.at[b, i - 1], p_s.at[b], p_r.at[b], dp, peer).start()

        @pl.loop(0, TILES)
        def _(j):
            tile = pl.ds(pl.multiple_of(j * W, W), W)
            total[:, tile] += lax.dot_general(
                a, units[b, :, tile], (((0,), (0,)), ((), ())), preferred_element_type=jnp.float32
            )

    def reduce(b):
        wait(arrived.at[b], p_r.at[b])
        value = part[b, t].astype(jnp.float32)
        for i in range(T - 1):
            value += arrived[b, i].astype(jnp.float32)
        reduced[b] = value.astype(jnp.bfloat16)

        @pl.when(b != dp)
        def _():
            remote(reduced.at[b], columns(grads, dp), g_s.at[b], g_r.at[dp], b, t).start()

        @pl.when(b == dp)
        def _():
            pltpu.make_async_copy(reduced.at[b], columns(grads, dp), g_s.at[b]).start()

    def sides(k, do, column):
        @pl.when((k >= 0) & (k < Z) & (z - k >= 0))
        def _():
            do((z - k) * X + column)

        @pl.when((k > 0) & (z + k < Z))
        def _():
            do((z + k) * X + column)

    def forward(ref, b, up_s=z_s, down_s=d_s, rs=u_r):
        @pl.when((b < z * X) & (z < Z - 1))
        def _():
            up(ref, b, up_s, rs)

        @pl.when((b >= (z + 1) * X) & (z > 0))
        def _():
            down(ref, b, down_s, rs)

    def take(b):
        @pl.when((b != dp) & is_end(b))
        def _():
            wait(first(b), u_r.at[b])
            forward(first(b), b)
            cross(first(b), b)

        @pl.when((b != dp) & jnp.logical_not(is_end(b)))
        def _():
            wait(whole(b), u_r.at[b])
            forward(whole(b), b)
            cross(whole(b), b)

    def is_split(b):
        return is_end(b) & (b // X != z)

    def compute_whole(b):
        @pl.when(jnp.logical_not(is_split(b)))
        def _():
            compute(b)

    def across_first(b):
        wait(whole(b), u_r.at[b])

        @pl.when(z == 0)
        def _():
            up(second(b), b, b_s, v_r)

        @pl.when(z == Z - 1)
        def _():
            down(second(b), b, b_s, v_r)

    def across_whole(b):
        @pl.when(jnp.logical_not(is_split(b)))
        def _():
            @pl.when(b // X != z)
            def _():
                wait(whole(b), u_r.at[b])

            compute(b)

    def at_last(do):
        def run(b):
            @pl.when((z == 0) | (z == Z - 1))
            def _():
                do(b)
        return run

    def before_last(do):
        def run(b):
            @pl.when((z > 0) & (z < Z - 1))
            def _():
                do(b)
        return run

    def take_second(b):
        @pl.when(is_split(b))
        def _():
            wait(second(b), v_r.at[b])
            forward(second(b), b, b_s, b_s, v_r)

    def compute_split(b):
        @pl.when(is_split(b))
        def _():
            compute(b)

    def across_split(b):
        @pl.when(is_split(b))
        def _():
            wait(first(b), u_r.at[b])
            compute(b)

    @pl.loop(0, Z + 2)
    def _(k):
        sides(k, take, x)

        @pl.when(k == 1)
        def _():
            across_first(z * X + (1 - x))

        sides(k, compute_whole, x)

        @pl.when((k == 0) & (z == 0))
        def _():
            wait(first(dp), z_s.at[dp])
            up(second(dp), dp, b_s, v_r)

        @pl.when((k == 0) & (z == Z - 1))
        def _():
            wait(first(dp), d_s.at[dp])
            down(second(dp), dp, b_s, v_r)

        sides(k - 1, across_whole, 1 - x)
        sides(k, take_second, x)
        sides(k, at_last(compute_split), x)
        sides(k, take_second, 1 - x)
        sides(k, before_last(compute_split), x)
        sides(k - 1, across_split, 1 - x)
        sides(k - 1, reduce, x)
        sides(k - 2, reduce, 1 - x)

    out_tiles = TILES

    @pl.loop(0, out_tiles)
    def _(j):
        tile = pl.ds(pl.multiple_of(j * W, W), W)
        wide[:, tile] = (total[:, tile] / DP).astype(jnp.bfloat16)

    out_w = pltpu.make_async_copy(wide, wg_out, loc.at[0])
    out_w.start()

    @pl.loop(0, DP)
    def _(b):
        @pl.when(b != dp)
        def _():
            wait(columns(grads, b), g_r.at[b])

        wait(reduced.at[b], g_s.at[b])
        wait(arrived.at[b], p_s.at[b])

    out_i = pltpu.make_async_copy(grads, ig_out, loc.at[1])
    out_i.start()

    @pl.loop(1, DP)
    def _(i):
        wait(cols.at[0, 0], in1_s.at[(dp + i) % DP])

    @pl.loop(1, T)
    def _(i):
        wait(cols.at[:, 0], in2_s.at[(t + i) % T])

    def sent(b, cond, sem, split):
        @pl.when(cond & split)
        def _():
            wait(first(b), sem.at[b])

        @pl.when(cond & jnp.logical_not(split))
        def _():
            wait(whole(b), sem.at[b])

    @pl.loop(0, Z)
    def _(c):
        b = c * X + x
        sent(b, c >= 0, x_s, is_split(b))
        sent(b, (c <= z) & (z < Z - 1) & (z + c > 0), z_s, is_end(b))
        sent(b, (c >= z) & (z > 0) & (z + c < 2 * Z - 2), d_s, is_end(b))

    @pl.loop(0, X)
    def _(c):
        @pl.when(z < Z - 1)
        def _():
            wait(second(c), b_s.at[c])

        @pl.when(z > 0)
        def _():
            wait(second(DP - X + c), b_s.at[DP - X + c])

    out_w.wait()
    out_i.wait()


def body(inputs, membrane, spike_grad, decay, gate_weight):
    DP, T = lax.axis_size("dp"), lax.axis_size("tensor")
    steps, own, features = inputs.shape
    R, F = gate_weight.shape
    unit_grad = unit_gradients(membrane, spike_grad, decay)
    rows = steps * own * T
    unit = unit_grad.reshape(steps, T, own, F).transpose(1, 0, 2, 3).reshape(rows, F)
    inp = inputs.reshape(steps * own, features)
    bf, f32 = jnp.bfloat16, jnp.float32
    dma = pltpu.SemaphoreType.DMA
    ig, wg = pl.pallas_call(
        functools.partial(kernel, DP, T),
        out_shape=(
            jax.ShapeDtypeStruct((steps * own, features), bf),
            jax.ShapeDtypeStruct((R, F), bf),
        ),
        in_specs=[pl.BlockSpec(memory_space=pl.ANY)] * 3,
        out_specs=(pl.BlockSpec(memory_space=pl.ANY),) * 2,
        scratch_shapes=[
            pltpu.VMEM((DP, rows, F), bf),
            pltpu.VMEM((DP, T, rows // T, R), bf),
            pltpu.VMEM((R, F), bf),
            pltpu.VMEM((R, F), f32),
            pltpu.VMEM((rows, R), f32),
            pltpu.VMEM((DP, T, rows // T, R), bf),
            pltpu.VMEM((DP, T - 1, rows // T, R), bf),
            pltpu.VMEM((DP, rows // T, R), bf),
            pltpu.VMEM((steps * own, features), bf),
            pltpu.VMEM((R, F), bf),
            dma((3,)), dma((DP,)), dma((DP,)), dma((T,)), dma((T,)),
            dma((DP,)), dma((DP,)), dma((DP,)), dma((DP,)), dma((DP,)), dma((DP,)),
            dma((DP,)), dma((DP,)), dma((DP,)), dma((DP,)),
        ],
        compiler_params=pltpu.CompilerParams(
            collective_id=0, has_side_effects=True, vmem_limit_bytes=56 * 1024 * 1024
        ),
        cost_estimate=pl.CostEstimate(
            flops=4 * DP * rows * R * F, bytes_accessed=4 * R * F + 2 * rows * F, transcendentals=0
        ),
    )(inp, unit, gate_weight)
    return (ig.reshape(steps, own, features), wg)


def solution(mesh):
    return jax.shard_map(
        body,
        mesh=mesh,
        in_specs=(
            P(None, ("dp", "tensor"), None),
            P(None, "dp", "tensor"),
            P(None, "dp", "tensor"),
            P("tensor"),
            P("dp", "tensor"),
        ),
        out_specs=(P(None, ("dp", "tensor"), None), P("dp", "tensor")),
        check_vma=False,
    )
```
